32 devices in a mesh: feat: 8 (over z, y), ex: 4 (over x, core).
Axes of the slice: x: 2, y: 2, z: 4, core: 2. Of those that a mesh axis runs over, the one named last changes fastest.
Arguments:
- activations: bfloat16 [1024, 28672], P('ex', 'feat'), may hold values from -6 to 6
- out_grads: bfloat16 [1024, 8192], P('feat', 'ex'), may hold values from -6 to 6
- basis_in: bfloat16 [28672, 28672], P('feat', 'ex'), may hold values from -0.03125 to 0.03125
- basis_out: bfloat16 [8192, 8192], P('ex', 'feat'), may hold values from -0.0625 to 0.0625
Outputs:
- correction: float32 [8192, 28672], P('feat', 'ex')
The draws below stay inside these ranges and needn't reach their ends.
All inputs are finite; a program needn't handle non-finite values.
Results may differ from the reference program's by a relative error of at most 0.0034.
Values may be sent and summed in bfloat16 or wider, within the bound.
No kernel may reach another device: no remote copies, remote signals or barrier semaphores. Data moves between devices by JAX's collectives and lax.ppermute only.
A program may use at most 192 MiB of HBM per device.

```python
import jax
import jax.numpy as jnp
from jax import lax

DIN = 28672
DOUT = 8192
SEQ_LEN = 256
SEQS = 4
TOKENS = 1024


def level_of(rng, extent, pieces, smallest, top_value):
    level = 1.0
    for position, parts in pieces:
        heights = jax.random.uniform(jax.random.fold_in(jax.random.fold_in(rng, 6), position), (parts,), jnp.float32, smallest / len(pieces), top_value / len(pieces))
        level = level * jnp.repeat(jnp.exp(heights), extent[position] // parts).reshape((-1,) + (1,) * (len(extent) - 1 - position))
    return level


def bell_draw(rng, dims, width, most, split=(), held_as=jnp.bfloat16):
    gain = level_of(rng, dims, split, -0.22, 0.18) if split else 1.0
    entries = jax.random.normal(rng, dims, jnp.float32) * width * gain
    return jnp.minimum(jnp.maximum(entries, -most), most).astype(held_as)


def setup_inputs(seed: int = 0) -> dict:
    splits = jax.random.split(jax.random.key(seed), 5)
    activations = bell_draw(splits[0], (TOKENS, DIN), 1.0, 6.0, ((0, 4), (1, 8)))
    out_grads = bell_draw(splits[1], (TOKENS, DOUT), 1.0, 6.0, ((0, 8), (1, 4)))
    basis_in = bell_draw(splits[2], (DIN, DIN), DIN ** -0.5, 0.03125, ((0, 8), (1, 4)))
    basis_out = bell_draw(splits[3], (DOUT, DOUT), DOUT ** -0.5, 0.0625, ((0, 4), (1, 8)))
    return {"activations": activations, "out_grads": out_grads, "basis_in": basis_in, "basis_out": basis_out}


def reference(activations, out_grads, basis_in, basis_out):
    rotated_in = jnp.dot(activations, basis_in, preferred_element_type=jnp.float32).astype(jnp.bfloat16)
    rotated_out = jnp.dot(out_grads, basis_out, preferred_element_type=jnp.float32).astype(jnp.bfloat16)
    in_blocks = rotated_in.reshape(SEQS, SEQ_LEN, DIN)
    out_blocks = rotated_out.reshape(SEQS, SEQ_LEN, DOUT)

    def accumulate(total, pair):
        per_seq = jnp.dot(pair[0].T, pair[1], preferred_element_type=jnp.float32)
        return total + per_seq * per_seq, None

    total, unused = lax.scan(accumulate, jnp.zeros((DOUT, DIN), jnp.float32), (out_blocks, in_blocks))
    return total / jnp.float32(TOKENS)
```

```python
import jax
import jax.numpy as jnp
from jax import lax
from jax.experimental import pallas as pl
from jax.experimental.pallas import tpu as pltpu
from jax.sharding import PartitionSpec as P

SEQ_LEN = 256
PARTS = 4
WIDTH = 256
BF16 = jnp.bfloat16
F32 = jnp.float32


def square_kernel(scale, out_t, p0, p1, p2, p3, *rest):
    result = rest[-1]
    total = None
    for n, piece in enumerate((p0, p1, p2, p3)):
        rows = piece.shape[0]
        for s in range(rows // SEQ_LEN):
            left = out_t[:, n * rows + s * SEQ_LEN : n * rows + (s + 1) * SEQ_LEN]
            right = piece[s * SEQ_LEN : (s + 1) * SEQ_LEN, :]
            product = jnp.dot(left, right, preferred_element_type=F32)
            total = product * product if total is None else total + product * product
    result[...] = total * scale


def square_into(buffer, out_t, pieces, first, width, full, scale):
    tile = 256
    rows = out_t.shape[0]
    depth = pieces[0].shape[0]
    offset = first // tile
    in_specs = [pl.BlockSpec(out_t.shape, lambda j: (0, 0))]
    in_specs += [pl.BlockSpec((depth, tile), lambda j: (0, j)) for _ in pieces]
    operands = [out_t, *pieces]
    aliases = {}
    if buffer is not None:
        in_specs.append(pl.BlockSpec(memory_space=pl.ANY))
        operands.append(buffer)
        aliases = {len(operands) - 1: 0}

    def body(*refs):
        square_kernel(scale, *refs)

    return pl.pallas_call(
        body,
        grid=(width // tile,),
        in_specs=in_specs,
        out_specs=pl.BlockSpec((rows, tile), lambda j: (0, offset + j)),
        out_shape=jax.ShapeDtypeStruct((rows, full), F32),
        input_output_aliases=aliases,
        compiler_params=pltpu.CompilerParams(vmem_limit_bytes=32 * 1024 * 1024),
        cost_estimate=pl.CostEstimate(
            flops=2 * rows * width * out_t.shape[1],
            bytes_accessed=rows * width * 4 + out_t.size * 2 + PARTS * depth * width * 2,
            transcendentals=0,
        ),
    )(*operands)


def call(kernel, flags, operands, in_specs, outputs, out_specs, grid, cost, aliases, vmem):
    return pl.pallas_call(
        kernel,
        grid_spec=pltpu.PrefetchScalarGridSpec(
            num_scalar_prefetch=1, grid=grid, in_specs=in_specs, out_specs=out_specs
        ),
        out_shape=outputs,
        input_output_aliases=aliases or {},
        compiler_params=pltpu.CompilerParams(vmem_limit_bytes=vmem * 1024 * 1024),
        cost_estimate=cost,
    )(flags, *operands)


def unit_list(count):
    lead = 6
    units = [[(0, i)] for i in range(4)] + [[(0, 4), (0, 5)]]
    units += [[(1, i), (1, i + 1)] for i in range(0, lead, 2)]
    rest = [(half, i) for i in range(lead, count) for half in (0, 1)]
    while rest:
        size = 2 if len(rest) > 8 else 1
        units.append(rest[:size])
        rest = rest[size:]
    return units


class Chain:
    def __init__(self, flags):
        self.flags = flags
        self.token = jnp.zeros((8, 128), F32)
        self.also = []

    def run(self, body, operands, in_specs, outputs, out_specs, grid, flops, size, aliases=None, vmem=12):
        waits = [self.token, *self.also]
        self.also = []
        count, made = len(operands), len(outputs)
        keep = pl.BlockSpec(memory_space=pl.ANY)

        def kernel(flags, *refs):
            refs[-1][...] = jnp.zeros((8, 128), F32)
            body(flags, refs[:count], refs[count + len(waits) : -1])

        results = call(
            kernel,
            self.flags,
            [*operands, *waits],
            [*in_specs, *[keep] * len(waits)],
            [*outputs, jax.ShapeDtypeStruct((8, 128), F32)],
            [*out_specs, pl.BlockSpec((8, 128), lambda *_: (0, 0))],
            grid,
            pl.CostEstimate(flops=flops, bytes_accessed=size, transcendentals=0),
            aliases,
            vmem,
        )
        self.token = results[made]
        return results[:made]


def multiply(chain, blocks, matrix, first, width, tile=256):
    rows = sum(block.shape[0] for block in blocks)
    inner = matrix.shape[0]
    base = first // tile

    def body(flags, ins, outs):
        (result,) = outs
        start = 0
        for block in ins[:-1]:
            here = slice(start, start + block.shape[0])
            start += block.shape[0]
            result[here, :] = jnp.dot(block[...], ins[-1][...], preferred_element_type=F32)

    return chain.run(
        body,
        [*blocks, matrix],
        [pl.BlockSpec(block.shape, lambda j, flags: (0, 0), pipeline_mode=pl.Buffered(1)) for block in blocks]
        + [pl.BlockSpec((inner, tile), lambda j, flags: (0, base + j))],
        [jax.ShapeDtypeStruct((rows, width), F32)],
        [pl.BlockSpec((rows, tile), lambda j, flags: (0, j))],
        (width // tile,),
        2 * rows * inner * width,
        2 * inner * (rows + width) + 4 * rows * width,
        vmem=18,
    )[0]


def relay(chain, value):
    tile = 128

    def body(flags, ins, outs):
        outs[0][...] = ins[0][...]

    spec = pl.BlockSpec((tile, value.shape[1]), lambda r, flags: (r, 0))
    shape = jax.ShapeDtypeStruct(value.shape, value.dtype)
    return chain.run(body, [value], [spec], [shape], [spec], (value.shape[0] // tile,), 0, 4 * value.size)[0]


def layout(parts):
    offsets, total = {}, 0
    for name, rows, present in parts:
        if present:
            offsets[name] = total
            total += rows
    return offsets, total


class Lane:
    def __init__(self, chain, units, permute):
        self.chain, self.units, self.permute = chain, units, permute
        self.sent, self.got, self.state, self.places, self.partials = {}, {}, {}, {}, {}

    def subs(self, u):
        return len(self.units[u]) if 0 <= u < len(self.units) else 0

    def advance(self, k, partials):
        half, n = SEQ_LEN, self.subs
        self.partials[k] = partials
        places, sizes = {}, {}
        for link, parts in (
            ("y", (("a1", half, n(k)), ("a5", half, n(k - 4)), ("b3", half, n(k - 2)))),
            ("z", (("za", half, max(n(k - 1), n(k - 3))), ("zb", 2 * half, max(n(k), n(k - 4))))),
            ("m", (("a3", half, n(k - 2)), ("b2", half, n(k - 1)), ("b4", half, n(k - 3)))),
        ):
            places[link], sizes[link] = layout([(name, rows * count, count) for name, rows, count in parts])
        before = self.places
        operands, in_specs, names, outputs, out_specs, out_names = [], [], [], [], [], []
        size = 0

        def read(name, array, rows=None, block=0, first=0):
            nonlocal size
            rows = rows or array.shape[0]
            base = first // 128
            operands.append(array)
            in_specs.append(pl.BlockSpec((rows, 128), lambda j, flags: (block, base + j)))
            names.append(name)
            size += rows * WIDTH * array.dtype.itemsize

        def write(name, rows, dtype):
            nonlocal size
            outputs.append(jax.ShapeDtypeStruct((rows, WIDTH), dtype))
            out_specs.append(pl.BlockSpec((rows, 128), lambda j, flags: (0, j)))
            out_names.append(name)
            size += rows * WIDTH * jnp.dtype(dtype).itemsize

        for link, array in self.got.items():
            read("got_" + link, array)
        for link, array in self.sent.items():
            if (link == "z" and (n(k - 4) or n(k - 5))) or (link == "m" and n(k - 4)):
                read("sent_" + link, array)
        for age in (0, 1):
            for s in range(n(k - age)):
                array, block, first = self.partials[k - age][s]
                read(f"p{age}a{s}", array, 2 * half, block, first)
                read(f"p{age}b{s}", array, 2 * half, block, first + WIDTH)
        for name, u in (("a1", k - 2), ("b1", k - 2), ("a2", k - 3), ("b2", k - 3)):
            if n(u):
                read("old_" + name, self.state[name])
        for link, rows in sizes.items():
            if rows:
                write("out_" + link, rows, BF16)
        for name, u in (("a1", k - 1), ("b1", k - 1), ("a2", k - 2), ("b2", k - 2)):
            if n(u):
                write("new_" + name, half * n(u), F32)
        if n(k - 5):
            write("final", 2 * half * n(k - 5), BF16)

        def body(flags, ins, outs):
            refs = dict(zip(names + out_names, (*ins, *outs)))
            y, side, outer = flags[0], flags[1], flags[2] == 1

            def rows(start, count=half):
                return pl.ds(pl.multiple_of(start, 16), count)

            def put(link, part, value, extra=0):
                start = places[link][part] + extra
                refs["out_" + link][start : start + value.shape[0], :] = value.astype(BF16)

            def take(kind, link, part, extra=0, count=half):
                return refs[kind + "_" + link][rows(before[link][part] + extra, count), :]

            for s in range(n(k)):
                put("y", "a1", refs[f"p0a{s}"][rows((1 - y) * half), :], s * half)
            for s in range(n(k - 1)):
                total = refs[f"p1a{s}"][rows(y * half), :] + take("got", "y", "a1", s * half).astype(F32)
                refs["new_a1"][s * half : (s + 1) * half, :] = total

            @pl.when(outer)
            def _():
                for s in range(n(k)):
                    put("z", "zb", refs[f"p0b{s}"][...], s * 2 * half)
                if n(k - 1):
                    put("z", "za", refs["new_a1"][...])
                if n(k - 4):
                    put("y", "a5", take("got", "z", "za", 0, half * n(k - 4)))
                if n(k - 5):
                    refs["final"][...] = take("got", "z", "zb", 0, 2 * half * n(k - 5))

            @pl.when(jnp.logical_not(outer))
            def _():
                for s in range(n(k - 1)):
                    for keep, start in ((False, (1 - side) * half), (True, side * half)):
                        value = refs[f"p1b{s}"][rows(start), :]
                        value += take("got", "z", "zb", start + s * 2 * half).astype(F32)
                        if keep:
                            refs["new_b1"][s * half : (s + 1) * half, :] = value
                        else:
                            put("m", "b2", value, s * half)
                if n(k - 2):
                    whole = half * n(k - 2)
                    total = refs["old_a1"][...] + take("got", "z", "za", 0, whole).astype(F32)
                    put("m", "a3", total)
                    refs["new_a2"][...] = total
                    total = refs["old_b1"][...] + take("got", "m", "b2", 0, whole).astype(F32)
                    put("y", "b3", total)
                    refs["new_b2"][...] = total
                if n(k - 3):
                    whole = half * n(k - 3)
                    put("z", "za", refs["old_a2"][...] + take("got", "m", "a3", 0, whole).astype(F32))
                    put("m", "b4", refs["old_b2"][...] + take("got", "y", "b3", 0, whole).astype(F32))
                if n(k - 4):
                    put("y", "a5", take("sent", "z", "za", 0, half * n(k - 4)))
                for s in range(n(k - 4)):
                    put("z", "zb", take("sent", "m", "b4", s * half), s * 2 * half)
                    put("z", "zb", take("got", "m", "b4", s * half), s * 2 * half + half)
                if n(k - 5):
                    refs["final"][...] = take("sent", "z", "zb", 0, 2 * half * n(k - 5))

        made = self.chain.run(body, operands, in_specs, outputs, out_specs, (WIDTH // 128,), 0, size, vmem=4 + size // 2**20 * 5 // 4)
        made = dict(zip(out_names, made))
        ready = []
        for s in range(n(k - 5)):
            place = before["y"]["a5"] // half + s
            ready.append((self.units[k - 5][s], (self.sent["y"], self.got["y"], place, made["final"], s)))
        self.places = places
        self.sent = {link: made["out_" + link] for link in sizes if sizes[link]}
        self.got = {link: self.permute[link](value) for link, value in self.sent.items()}
        self.state = {name[4:]: value for name, value in made.items() if name.startswith("new_")}
        return ready


def square_chunk(chain, buffer, out_t, pair, index, full, scale):
    rows = out_t.shape[1]
    tile = 512
    operands, in_specs = [out_t], [pl.BlockSpec((PARTS, tile, SEQ_LEN), lambda r, flags: (0, r, 0))]
    for own, other, place, _, _ in pair:
        for array in (own, other):
            operands.append(array)
            in_specs.append(pl.BlockSpec((SEQ_LEN, WIDTH), lambda r, flags, place=place: (place, 0)))
    for *_, final, s in pair:
        operands.append(final)
        in_specs.append(pl.BlockSpec((2 * SEQ_LEN, WIDTH), lambda r, flags, s=s: (s, 0)))
    aliases = {}
    if buffer is not None:
        in_specs.append(pl.BlockSpec(memory_space=pl.ANY))
        operands.append(buffer)
        aliases = {len(operands): 0}

    def body(flags, ins, outs):
        y, side = flags[0], flags[1]
        left, a, b = ins[0], ins[1:5], ins[5:7]
        (result,) = outs

        def square(seq, right):
            product = jnp.dot(left[seq], right, preferred_element_type=F32)
            return product * product

        total = square(y, a[0][...]) + square(1 - y, a[1][...])
        total += square(2 + y, a[2][...]) + square(3 - y, a[3][...])
        result[:, :WIDTH] = total * scale
        total = square(side, b[0][:SEQ_LEN, :]) + square(1 - side, b[0][SEQ_LEN:, :])
        total += square(2 + side, b[1][:SEQ_LEN, :]) + square(3 - side, b[1][SEQ_LEN:, :])
        result[:, WIDTH:] = total * scale

    return chain.run(
        body,
        operands,
        in_specs,
        [jax.ShapeDtypeStruct((rows, full), F32)],
        [pl.BlockSpec((tile, 2 * WIDTH), lambda r, flags: (r, index))],
        (rows // tile,),
        4 * rows * WIDTH * PARTS * SEQ_LEN,
        rows * WIDTH * 8 + out_t.size * 2 + PARTS * SEQ_LEN * WIDTH * 4,
        aliases,
    )[0]


def make_per_device(feat, ex):
    depth = feat // 2
    mid = depth // 2

    def along_z(pairs):
        return [(a * 2 + y, b * 2 + y) for a, b in pairs for y in (0, 1)]

    inward = [along_z([(k, k + 1), (depth - 1 - k, depth - 2 - k)]) for k in range(mid - 1)]
    outward = [along_z([(k + 1, k), (depth - 2 - k, depth - 1 - k)]) for k in reversed(range(mid - 1))]
    middle = along_z([(mid - 1, mid), (mid, mid - 1)])
    y_swap = [(i, i ^ 1) for i in range(feat)]
    y_middle = [(i, i ^ 1) for i in range(feat) if i // 2 in (mid - 1, mid)]

    def swap_ex(value, bit):
        return lax.ppermute(value, "ex", [(i, i ^ bit) for i in range(ex)])

    def send(value, pairs):
        return lax.ppermute(value.astype(BF16), "feat", pairs)

    def gather_low(block):
        bit = 1
        while bit < ex // 2:
            block = jnp.concatenate([block, swap_ex(block, bit)], axis=0)
            bit *= 2
        return block

    def spread(value, z):
        for step, pairs in enumerate(outward):
            level = mid - 2 - step
            here = (z == level) | (z == depth - 1 - level)
            value = jnp.where(here, lax.ppermute(value, "feat", pairs), value)
        return value

    def tree_a(partial, y, z):
        half = partial.shape[0] // 2
        away = lax.dynamic_slice_in_dim(partial, (1 - y) * half, half, 0)
        total = lax.dynamic_slice_in_dim(partial, y * half, half, 0)
        total = total + send(away, y_swap).astype(F32)
        for pairs in inward:
            total = total + send(total, pairs).astype(F32)
        total = (total + send(total, middle).astype(F32)).astype(BF16)
        total = spread(total, z)
        return [total, lax.ppermute(total, "feat", y_swap)]

    def tree_b(partial, side, z):
        half = partial.shape[0] // 2
        for pairs in inward:
            partial = partial + send(partial, pairs).astype(F32)
        away = lax.dynamic_slice_in_dim(partial, (1 - side) * half, half, 0)
        total = lax.dynamic_slice_in_dim(partial, side * half, half, 0)
        total = total + send(away, middle).astype(F32)
        total = (total + send(total, y_middle).astype(F32)).astype(BF16)
        other = lax.ppermute(total, "feat", middle)
        return [spread(total, z), spread(other, z)]

    def pipelined(activations, out_grads, basis_in, basis_out, flags, ordered):
        columns = basis_in.shape[1]
        chain = Chain(flags)
        stay = [(k, k) for k in range(feat) if k // 2 in (0, depth - 1)]
        permute = {
            "y": lambda v: lax.ppermute(v, "feat", y_swap),
            "z": lambda v: lax.ppermute(v, "feat", inward[0] + outward[0]),
            "m": lambda v: lax.ppermute(v, "feat", middle + stay),
        }
        near = [activations, swap_ex(activations, 1)]
        far = swap_ex(activations, 2)
        grad_all = lax.all_gather(out_grads, "feat", axis=0, tiled=True)
        tokens_all = PARTS * activations.shape[0]
        tokens = [near, None]

        count = columns // (2 * WIDTH)
        units = unit_list(count)
        lanes = [Lane(chain, units[p::2], permute) for p in (0, 1)]
        finished, made = {}, {}
        result = rotated_out = out_t = None
        for j in range(len(units) + 12):
            lane, k = lanes[j % 2], j // 2
            if k >= len(lane.units) + 6:
                continue
            partials = None
            if lane.subs(k):
                unit = lane.units[k]
                if tokens[1] is None and j == 4:
                    far = relay(chain, far)
                    tokens[1] = [far, swap_ex(far, 1)]
                if unit[0] not in made:
                    group = list(unit)
                    if j + 1 < len(units) and len({half for half, _ in unit + units[j + 1]}) == len(unit) == 2:
                        if len({i for _, i in unit}) == 1:
                            group += units[j + 1]
                    halves = sorted({half for half, _ in group})
                    chunks = sorted({i for _, i in group})
                    blocks = [block for half in halves for block in tokens[half]]
                    wide = 2 * WIDTH * len(chunks)
                    array = multiply(chain, blocks, basis_in, chunks[0] * 2 * WIDTH, wide)
                    for half, i in group:
                        made[half, i] = (array, halves.index(half), chunks.index(i) * 2 * WIDTH)
                partials = [made[sub] for sub in unit]
            ready = lane.advance(k, partials)
            other = lanes[1 - j % 2].got
            if len(other) == 3 and len(lane.got) == 3:
                chain.also.append(other["m"])
            if j == 6:
                share = multiply(chain, [grad_all], basis_out, 0, basis_out.shape[1])
                share = lax.psum_scatter(share, "ex", scatter_dimension=0, tiled=True)
                rotated_out = lax.all_gather(share.astype(BF16), "ex", axis=0, tiled=True)
            if j == 14:
                out_t = ordered(rotated_out, 0).reshape(-1, PARTS, SEQ_LEN).transpose(1, 0, 2)
                chain.also.append(out_t)
            for (half, i), value in ready:
                finished[half, i] = value
                if (1 - half, i) in finished:
                    pair = (finished[0, i], finished[1, i])
                    result = square_chunk(chain, result, out_t, pair, i, columns, 1.0 / tokens_all)
        return result

    def per_device(activations, out_grads, basis_in, basis_out):
        place = lax.axis_index("feat")
        e = lax.axis_index("ex")
        y, z = place % 2, place // 2
        side = (z >= mid).astype(jnp.int32)
        columns = basis_in.shape[1]

        block = activations.shape[0]

        def ordered(rotated_out, flip):
            turned = []
            for q in range(PARTS):
                for r in range(ex // PARTS):
                    source = e ^ ((q ^ flip) * (ex // PARTS) + r)
                    turned.append(lax.dynamic_slice_in_dim(rotated_out, source * block, block, 0))
            return jnp.concatenate(turned, axis=0).T

        if depth == 4 and ex == PARTS and block == SEQ_LEN and columns % (2 * WIDTH) == 0:
            outer = ((z == 0) | (z == depth - 1)).astype(jnp.int32)
            flags = jnp.stack([y.astype(jnp.int32), side, outer])
            return pipelined(activations, out_grads, basis_in, basis_out, flags, ordered)

        far = swap_ex(activations, ex // 2)
        tokens_half = [gather_low(activations), gather_low(far)]
        tokens_all = 2 * tokens_half[0].shape[0]
        scale = 1.0 / tokens_all
        grad_all = lax.all_gather(out_grads, "feat", axis=0, tiled=True)
        out_share = lax.psum_scatter(
            jnp.dot(grad_all, basis_out, preferred_element_type=F32),
            "ex",
            scatter_dimension=0,
            tiled=True,
        )
        rotated_out = lax.all_gather(out_share.astype(BF16), "ex", axis=0, tiled=True)
        out_a, out_b = ordered(rotated_out, y), ordered(rotated_out, side)

        width = 512
        chunks = list(range(0, columns, width))
        lead = 4
        order = [(0, i) for i in range(min(lead, len(chunks)))]
        for i in range(len(chunks)):
            order.append((1, i))
            if i + lead < len(chunks):
                order.append((0, i + lead))
        pieces = {}
        result = None
        for half, i in order:
            first = chunks[i]
            partial = jnp.dot(tokens_half[half], basis_in[:, first : first + width], preferred_element_type=F32)
            if i % 2 == 0:
                pieces[half, i] = tree_a(partial, y, z)
            else:
                pieces[half, i] = tree_b(partial, side, z)
            if half == 1:
                result = square_into(
                    result, out_a if i % 2 == 0 else out_b, pieces[0, i] + pieces[1, i], first, width, columns, scale
                )
        return result

    return per_device


def solution(mesh):
    return jax.shard_map(
        make_per_device(mesh.shape["feat"], mesh.shape["ex"]),
        mesh=mesh,
        in_specs=(P("ex", "feat"), P("feat", "ex"), P("feat", "ex"), P("ex", "feat")),
        out_specs=P("feat", "ex"),
        check_vma=False,
    )
```

```python
import jax
import jax.numpy as jnp
from jax import lax
from jax.experimental import pallas as pl
from jax.experimental.pallas import tpu as pltpu
from jax.sharding import PartitionSpec as P

SEQ_LEN = 256
EXTRA = {0: 1, 1: 1, 2: 1, 3: 1, 4: 1, 9: 1, 10: 1, 11: 1, 12: 1, 13: 2, 14: 1}
PARTS = 4
WIDTH = 256
BF16 = jnp.bfloat16
F32 = jnp.float32


def square_kernel(scale, out_t, p0, p1, p2, p3, *rest):
    result = rest[-1]
    total = None
    for n, piece in enumerate((p0, p1, p2, p3)):
        rows = piece.shape[0]
        for s in range(rows // SEQ_LEN):
            left = out_t[:, n * rows + s * SEQ_LEN : n * rows + (s + 1) * SEQ_LEN]
            right = piece[s * SEQ_LEN : (s + 1) * SEQ_LEN, :]
            product = jnp.dot(left, right, preferred_element_type=F32)
            total = product * product if total is None else total + product * product
    result[...] = total * scale


def square_into(buffer, out_t, pieces, first, width, full, scale):
    tile = 256
    rows = out_t.shape[0]
    depth = pieces[0].shape[0]
    offset = first // tile
    in_specs = [pl.BlockSpec(out_t.shape, lambda j: (0, 0))]
    in_specs += [pl.BlockSpec((depth, tile), lambda j: (0, j)) for _ in pieces]
    operands = [out_t, *pieces]
    aliases = {}
    if buffer is not None:
        in_specs.append(pl.BlockSpec(memory_space=pl.ANY))
        operands.append(buffer)
        aliases = {len(operands) - 1: 0}

    def body(*refs):
        square_kernel(scale, *refs)

    return pl.pallas_call(
        body,
        grid=(width // tile,),
        in_specs=in_specs,
        out_specs=pl.BlockSpec((rows, tile), lambda j: (0, offset + j)),
        out_shape=jax.ShapeDtypeStruct((rows, full), F32),
        input_output_aliases=aliases,
        compiler_params=pltpu.CompilerParams(vmem_limit_bytes=32 * 1024 * 1024),
        cost_estimate=pl.CostEstimate(
            flops=2 * rows * width * out_t.shape[1],
            bytes_accessed=rows * width * 4 + out_t.size * 2 + PARTS * depth * width * 2,
            transcendentals=0,
        ),
    )(*operands)


def call(kernel, flags, operands, in_specs, outputs, out_specs, grid, cost, aliases, vmem):
    return pl.pallas_call(
        kernel,
        grid_spec=pltpu.PrefetchScalarGridSpec(
            num_scalar_prefetch=1, grid=grid, in_specs=in_specs, out_specs=out_specs
        ),
        out_shape=outputs,
        input_output_aliases=aliases or {},
        compiler_params=pltpu.CompilerParams(vmem_limit_bytes=vmem * 1024 * 1024),
        cost_estimate=cost,
    )(flags, *operands)


def unit_list(count):
    lead = 6
    units = [[(0, i)] for i in range(lead)]
    units += [[(1, i), (1, i + 1)] for i in range(0, lead, 2)]
    rest = [(half, i) for i in range(lead, count) for half in (0, 1)]
    while rest:
        size = 2 if len(rest) > 4 else 1
        units.append(rest[:size])
        rest = rest[size:]
    return units


class Chain:
    def __init__(self, flags):
        self.flags = flags
        self.token = jnp.zeros((8, 128), F32)
        self.also = []

    def run(self, body, operands, in_specs, outputs, out_specs, grid, flops, size, aliases=None, vmem=10):
        waits = [self.token, *self.also]
        self.also = []
        count, made = len(operands), len(outputs)
        keep = pl.BlockSpec(memory_space=pl.ANY)

        def kernel(flags, *refs):
            refs[-1][...] = jnp.zeros((8, 128), F32)
            body(flags, refs[:count], refs[count + len(waits) : -1])

        results = call(
            kernel,
            self.flags,
            [*operands, *waits],
            [*in_specs, *[keep] * len(waits)],
            [*outputs, jax.ShapeDtypeStruct((8, 128), F32)],
            [*out_specs, pl.BlockSpec((8, 128), lambda *_: (0, 0))],
            grid,
            pl.CostEstimate(flops=flops, bytes_accessed=size, transcendentals=0),
            aliases,
            vmem,
        )
        self.token = results[made]
        return results[:made]


def multiply(chain, blocks, matrix, first, width, dtype, vmem, tile=256):
    rows = sum(block.shape[0] for block in blocks)
    inner = matrix.shape[0]
    base = first // tile

    def body(flags, ins, outs):
        (result,) = outs
        start = 0
        for block in ins[:-1]:
            here = slice(start, start + block.shape[0])
            start += block.shape[0]
            result[here, :] = jnp.dot(block[...], ins[-1][...], preferred_element_type=F32).astype(dtype)

    return chain.run(
        body,
        [*blocks, matrix],
        [pl.BlockSpec(block.shape, lambda j, flags: (0, 0), pipeline_mode=pl.Buffered(1)) for block in blocks]
        + [pl.BlockSpec((inner, tile), lambda j, flags: (0, base + j))],
        [jax.ShapeDtypeStruct((rows, width), dtype)],
        [pl.BlockSpec((rows, tile), lambda j, flags: (0, j))],
        (width // tile,),
        2 * rows * inner * width,
        2 * inner * (rows + width) + 4 * rows * width,
        vmem=vmem,
    )[0]


def relay(chain, value):
    tile = 128

    def body(flags, ins, outs):
        outs[0][...] = ins[0][...]

    spec = pl.BlockSpec((tile, value.shape[1]), lambda r, flags: (r, 0))
    shape = jax.ShapeDtypeStruct(value.shape, value.dtype)
    return chain.run(body, [value], [spec], [shape], [spec], (value.shape[0] // tile,), 0, 4 * value.size)[0]


def rotate_out(chain, grads, basis):
    inner, width = basis.shape
    tile = 256

    def body(flags, ins, outs):
        for q in range(PARTS):
            rows = pl.ds(pl.multiple_of((flags[3] ^ q) * SEQ_LEN, SEQ_LEN), SEQ_LEN)
            product = jnp.dot(ins[0][rows, :], ins[1][...], preferred_element_type=F32)
            outs[q % 2][q // 2 * SEQ_LEN : (q // 2 + 1) * SEQ_LEN, :] = product

    half = jax.ShapeDtypeStruct((2 * SEQ_LEN, width), F32)
    return chain.run(
        body,
        [grads, basis],
        [
            pl.BlockSpec(grads.shape, lambda j, flags: (0, 0), pipeline_mode=pl.Buffered(1)),
            pl.BlockSpec((inner, tile), lambda j, flags: (0, j)),
        ],
        [half, half],
        [pl.BlockSpec((2 * SEQ_LEN, tile), lambda j, flags: (0, j))] * 2,
        (width // tile,),
        2 * grads.size * width,
        2 * (grads.size + basis.size) + 4 * PARTS * SEQ_LEN * width,
        vmem=14,
    )


def add_rows(chain, mine, other, dtype):
    rows, width = mine.shape
    tile = 256
    count = rows // SEQ_LEN

    def body(flags, ins, outs):
        for n in range(count):
            here = slice(n * SEQ_LEN, (n + 1) * SEQ_LEN)
            outs[n][...] = (ins[0][here, :] + ins[1][here, :]).astype(dtype)

    return chain.run(
        body,
        [mine, other],
        [pl.BlockSpec((rows, tile), lambda j, flags: (0, j))] * 2,
        [jax.ShapeDtypeStruct((SEQ_LEN, width), dtype)] * count,
        [pl.BlockSpec((SEQ_LEN, tile), lambda j, flags: (0, j))] * count,
        (width // tile,),
        0,
        12 * rows * width,
    )


def turn(chain, pieces):
    rows, width = pieces[0].shape
    tile = 256

    def body(flags, ins, outs):
        for q in range(len(pieces)):
            outs[0][q] = ins[q][...].T

    return chain.run(
        body,
        pieces,
        [pl.BlockSpec((rows, tile), lambda j, flags: (0, j))] * len(pieces),
        [jax.ShapeDtypeStruct((len(pieces), width, rows), pieces[0].dtype)],
        [pl.BlockSpec((len(pieces), tile, rows), lambda j, flags: (0, j, 0))],
        (width // tile,),
        0,
        4 * len(pieces) * rows * width,
    )[0]


def layout(parts):
    offsets, total = {}, 0
    for name, rows, present in parts:
        if present:
            offsets[name] = total
            total += rows
    return offsets, total


class Lane:
    def __init__(self, chain, units, permute):
        self.chain, self.units, self.permute = chain, units, permute
        self.sent, self.got, self.state, self.places, self.partials = {}, {}, {}, {}, {}

    def subs(self, u):
        return len(self.units[u]) if 0 <= u < len(self.units) else 0

    def advance(self, k, partials):
        half, n = SEQ_LEN, self.subs
        self.partials[k] = partials
        places, sizes = {}, {}
        for link, parts in (
            ("y", (("a1", half, n(k)), ("a5", half, n(k - 4)), ("b3", half, n(k - 2)))),
            ("z", (("za", half, max(n(k - 1), n(k - 3))), ("zb", 2 * half, max(n(k), n(k - 4))))),
            ("m", (("a3", half, n(k - 2)), ("b2", half, n(k - 1)), ("b4", half, n(k - 3)))),
        ):
            places[link], sizes[link] = layout([(name, rows * count, count) for name, rows, count in parts])
        before = self.places
        operands, in_specs, names, outputs, out_specs, out_names = [], [], [], [], [], []
        size = 0

        def read(name, array, rows=None, block=0, first=0):
            nonlocal size
            rows = rows or array.shape[0]
            base = first // 128
            operands.append(array)
            in_specs.append(pl.BlockSpec((rows, 128), lambda j, flags: (block, base + j)))
            names.append(name)
            size += rows * WIDTH * array.dtype.itemsize

        def write(name, rows, dtype):
            nonlocal size
            outputs.append(jax.ShapeDtypeStruct((rows, WIDTH), dtype))
            out_specs.append(pl.BlockSpec((rows, 128), lambda j, flags: (0, j)))
            out_names.append(name)
            size += rows * WIDTH * jnp.dtype(dtype).itemsize

        for link, array in self.got.items():
            read("got_" + link, array)
        for link, array in self.sent.items():
            if (link == "z" and (n(k - 4) or n(k - 5))) or (link == "m" and n(k - 4)):
                read("sent_" + link, array)
        for age in (0, 1):
            for s in range(n(k - age)):
                array, block, first = self.partials[k - age][s]
                read(f"p{age}a{s}", array, 2 * half, block, first)
                read(f"p{age}b{s}", array, 2 * half, block, first + WIDTH)
        for name, u in (("a1", k - 2), ("b1", k - 2), ("a2", k - 3), ("b2", k - 3)):
            if n(u):
                read("old_" + name, self.state[name])
        for link, rows in sizes.items():
            if rows:
                write("out_" + link, rows, BF16)
        for name, u in (("a1", k - 1), ("b1", k - 1), ("a2", k - 2), ("b2", k - 2)):
            if n(u):
                write("new_" + name, half * n(u), F32)
        if n(k - 5):
            write("final", 2 * half * n(k - 5), BF16)

        def body(flags, ins, outs):
            refs = dict(zip(names + out_names, (*ins, *outs)))
            y, side, outer = flags[0], flags[1], flags[2] == 1

            def rows(start, count=half):
                return pl.ds(pl.multiple_of(start, 16), count)

            def put(link, part, value, extra=0):
                start = places[link][part] + extra
                refs["out_" + link][start : start + value.shape[0], :] = value.astype(BF16)

            def take(kind, link, part, extra=0, count=half):
                return refs[kind + "_" + link][rows(before[link][part] + extra, count), :]

            for s in range(n(k)):
                put("y", "a1", refs[f"p0a{s}"][rows((1 - y) * half), :], s * half)
            for s in range(n(k - 1)):
                total = refs[f"p1a{s}"][rows(y * half), :].astype(F32) + take("got", "y", "a1", s * half).astype(F32)
                refs["new_a1"][s * half : (s + 1) * half, :] = total

            @pl.when(outer)
            def _():
                for s in range(n(k)):
                    put("z", "zb", refs[f"p0b{s}"][...], s * 2 * half)
                if n(k - 1):
                    put("z", "za", refs["new_a1"][...])
                if n(k - 4):
                    put("y", "a5", take("got", "z", "za", 0, half * n(k - 4)))
                if n(k - 5):
                    refs["final"][...] = take("got", "z", "zb", 0, 2 * half * n(k - 5))

            @pl.when(jnp.logical_not(outer))
            def _():
                for s in range(n(k - 1)):
                    for keep, start in ((False, (1 - side) * half), (True, side * half)):
                        value = refs[f"p1b{s}"][rows(start), :].astype(F32)
                        value += take("got", "z", "zb", start + s * 2 * half).astype(F32)
                        if keep:
                            refs["new_b1"][s * half : (s + 1) * half, :] = value
                        else:
                            put("m", "b2", value, s * half)
                if n(k - 2):
                    whole = half * n(k - 2)
                    total = refs["old_a1"][...] + take("got", "z", "za", 0, whole).astype(F32)
                    put("m", "a3", total)
                    refs["new_a2"][...] = total
                    total = refs["old_b1"][...] + take("got", "m", "b2", 0, whole).astype(F32)
                    put("y", "b3", total)
                    refs["new_b2"][...] = total
                if n(k - 3):
                    whole = half * n(k - 3)
                    put("z", "za", refs["old_a2"][...] + take("got", "m", "a3", 0, whole).astype(F32))
                    put("m", "b4", refs["old_b2"][...] + take("got", "y", "b3", 0, whole).astype(F32))
                if n(k - 4):
                    put("y", "a5", take("sent", "z", "za", 0, half * n(k - 4)))
                for s in range(n(k - 4)):
                    put("z", "zb", take("sent", "m", "b4", s * half), s * 2 * half)
                    put("z", "zb", take("got", "m", "b4", s * half), s * 2 * half + half)
                if n(k - 5):
                    refs["final"][...] = take("sent", "z", "zb", 0, 2 * half * n(k - 5))

        made = self.chain.run(body, operands, in_specs, outputs, out_specs, (WIDTH // 128,), 0, size, vmem=4 + size // 2**20)
        made = dict(zip(out_names, made))
        ready = []
        for s in range(n(k - 5)):
            place = before["y"]["a5"] // half + s
            ready.append((self.units[k - 5][s], (self.sent["y"], self.got["y"], place, made["final"], s)))
        self.places = places
        self.sent = {link: made["out_" + link] for link in sizes if sizes[link]}
        self.got = {link: self.permute[link](value) for link, value in self.sent.items()}
        self.state = {name[4:]: value for name, value in made.items() if name.startswith("new_")}
        return ready


def square_chunk(chain, buffer, out_t, pair, index, full, scale):
    rows = out_t.shape[1]
    tile = 512
    operands, in_specs = [out_t], [pl.BlockSpec((PARTS, tile, SEQ_LEN), lambda r, flags: (0, r, 0))]
    for own, other, place, _, _ in pair:
        for array in (own, other):
            operands.append(array)
            in_specs.append(pl.BlockSpec((SEQ_LEN, WIDTH), lambda r, flags, place=place: (place, 0)))
    for *_, final, s in pair:
        operands.append(final)
        in_specs.append(pl.BlockSpec((2 * SEQ_LEN, WIDTH), lambda r, flags, s=s: (s, 0)))
    aliases = {}
    if buffer is not None:
        in_specs.append(pl.BlockSpec(memory_space=pl.ANY))
        operands.append(buffer)
        aliases = {len(operands): 0}

    def body(flags, ins, outs):
        y, side = flags[0], flags[1]
        left, a, b = ins[0], ins[1:5], ins[5:7]
        (result,) = outs

        def square(seq, right):
            product = jnp.dot(left[seq], right, preferred_element_type=F32)
            return product * product

        total = square(y, a[0][...]) + square(1 - y, a[1][...])
        total += square(2 + y, a[2][...]) + square(3 - y, a[3][...])
        result[:, :WIDTH] = total * scale
        total = square(side, b[0][:SEQ_LEN, :]) + square(1 - side, b[0][SEQ_LEN:, :])
        total += square(2 + side, b[1][:SEQ_LEN, :]) + square(3 - side, b[1][SEQ_LEN:, :])
        result[:, WIDTH:] = total * scale

    return chain.run(
        body,
        operands,
        in_specs,
        [jax.ShapeDtypeStruct((rows, full), F32)],
        [pl.BlockSpec((tile, 2 * WIDTH), lambda r, flags: (r, index))],
        (rows // tile,),
        4 * rows * WIDTH * PARTS * SEQ_LEN,
        rows * WIDTH * 8 + out_t.size * 2 + PARTS * SEQ_LEN * WIDTH * 4,
        aliases,
    )[0]


def make_per_device(feat, ex):
    depth = feat // 2
    mid = depth // 2

    def along_z(pairs):
        return [(a * 2 + y, b * 2 + y) for a, b in pairs for y in (0, 1)]

    inward = [along_z([(k, k + 1), (depth - 1 - k, depth - 2 - k)]) for k in range(mid - 1)]
    outward = [along_z([(k + 1, k), (depth - 2 - k, depth - 1 - k)]) for k in reversed(range(mid - 1))]
    middle = along_z([(mid - 1, mid), (mid, mid - 1)])
    y_swap = [(i, i ^ 1) for i in range(feat)]
    y_middle = [(i, i ^ 1) for i in range(feat) if i // 2 in (mid - 1, mid)]

    def swap_ex(value, bit):
        return lax.ppermute(value, "ex", [(i, i ^ bit) for i in range(ex)])

    def send(value, pairs):
        return lax.ppermute(value.astype(BF16), "feat", pairs)

    def gather_low(block):
        bit = 1
        while bit < ex // 2:
            block = jnp.concatenate([block, swap_ex(block, bit)], axis=0)
            bit *= 2
        return block

    def spread(value, z):
        for step, pairs in enumerate(outward):
            level = mid - 2 - step
            here = (z == level) | (z == depth - 1 - level)
            value = jnp.where(here, lax.ppermute(value, "feat", pairs), value)
        return value

    def tree_a(partial, y, z):
        half = partial.shape[0] // 2
        away = lax.dynamic_slice_in_dim(partial, (1 - y) * half, half, 0)
        total = lax.dynamic_slice_in_dim(partial, y * half, half, 0)
        total = total + send(away, y_swap).astype(F32)
        for pairs in inward:
            total = total + send(total, pairs).astype(F32)
        total = (total + send(total, middle).astype(F32)).astype(BF16)
        total = spread(total, z)
        return [total, lax.ppermute(total, "feat", y_swap)]

    def tree_b(partial, side, z):
        half = partial.shape[0] // 2
        for pairs in inward:
            partial = partial + send(partial, pairs).astype(F32)
        away = lax.dynamic_slice_in_dim(partial, (1 - side) * half, half, 0)
        total = lax.dynamic_slice_in_dim(partial, side * half, half, 0)
        total = total + send(away, middle).astype(F32)
        total = (total + send(total, y_middle).astype(F32)).astype(BF16)
        other = lax.ppermute(total, "feat", middle)
        return [spread(total, z), spread(other, z)]

    def pipelined(activations, out_grads, basis_in, basis_out, flags):
        columns = basis_in.shape[1]
        chain = Chain(flags)
        stay = [(k, k) for k in range(feat) if k // 2 in (0, depth - 1)]
        permute = {
            "y": lambda v: lax.ppermute(v, "feat", y_swap),
            "z": lambda v: lax.ppermute(v, "feat", inward[0] + outward[0]),
            "m": lambda v: lax.ppermute(v, "feat", middle + stay),
        }
        near = [activations, swap_ex(activations, 1)]
        far = swap_ex(activations, 2)
        grad_all = lax.all_gather(out_grads, "feat", axis=0, tiled=True)
        tokens_all = PARTS * activations.shape[0]
        tokens = [near, None]

        count = columns // (2 * WIDTH)
        units = unit_list(count)
        lanes = [Lane(chain, units[p::2], permute) for p in (0, 1)]
        finished, made, waiting = {}, {}, []

        def square(result, i):
            pair = (finished[0, i], finished[1, i])
            return square_chunk(chain, result, out_t, pair, i, columns, 1.0 / tokens_all)

        result = out_t = None
        for j in range(len(units) + 12):
            lane, k = lanes[j % 2], j // 2
            if k >= len(lane.units) + 6:
                continue
            partials = None
            if lane.subs(k):
                unit = lane.units[k]
                if tokens[1] is None and j == 4:
                    far = relay(chain, far)
                    tokens[1] = [far, swap_ex(far, 1)]
                if unit[0] not in made:
                    group = list(unit)
                    if j + 1 < len(units) and len({half for half, _ in unit + units[j + 1]}) == len(unit) == 2:
                        if len({i for _, i in unit}) == 1:
                            group += units[j + 1]
                    halves = sorted({half for half, _ in group})
                    chunks = sorted({i for _, i in group})
                    blocks = [block for half in halves for block in tokens[half]]
                    wide = 2 * WIDTH * len(chunks)
                    array = multiply(chain, blocks, basis_in, chunks[0] * 2 * WIDTH, wide, BF16, 8 if len(blocks) == 2 else 14)
                    for half, i in group:
                        made[half, i] = (array, halves.index(half), chunks.index(i) * 2 * WIDTH)
                partials = [made[sub] for sub in unit]
            ready = lane.advance(k, partials)
            other = lanes[1 - j % 2].got
            spare = len(lane.got) + len(other) + EXTRA.get(j, 0) - 5
            chain.also += [other[link] for link in "myz" if link in other][: max(spare, 0)]
            if j == 9:
                keep, away = rotate_out(chain, grad_all, basis_out)
                away = swap_ex(away, 1)
            if j == 10:
                keep, away = add_rows(chain, keep, away, F32)
                away = swap_ex(away, 2)
            if j == 13:
                (own,) = add_rows(chain, keep, away, BF16)
                across = swap_ex(own, 2)
                beside = [swap_ex(own, 1), swap_ex(across, 1)]
            if j == 15:
                out_t = turn(chain, [own, beside[0], across, beside[1]])
            for (half, i), value in ready:
                finished[half, i] = value
                if (1 - half, i) in finished:
                    waiting.append(i)
            if waiting and out_t is not None:
                result = square(result, waiting.pop(0))
        for i in waiting:
            result = square(result, i)
        return result

    def per_device(activations, out_grads, basis_in, basis_out):
        place = lax.axis_index("feat")
        e = lax.axis_index("ex")
        y, z = place % 2, place // 2
        side = (z >= mid).astype(jnp.int32)
        columns = basis_in.shape[1]

        block = activations.shape[0]

        def ordered(rotated_out, flip):
            turned = []
            for q in range(PARTS):
                for r in range(ex // PARTS):
                    source = e ^ ((q ^ flip) * (ex // PARTS) + r)
                    turned.append(lax.dynamic_slice_in_dim(rotated_out, source * block, block, 0))
            return jnp.concatenate(turned, axis=0).T

        if depth == 4 and ex == PARTS and block == SEQ_LEN and columns % (2 * WIDTH) == 0:
            outer = ((z == 0) | (z == depth - 1)).astype(jnp.int32)
            flags = jnp.stack([y.astype(jnp.int32), side, outer, e.astype(jnp.int32)])
            return pipelined(activations, out_grads, basis_in, basis_out, flags)

        far = swap_ex(activations, ex // 2)
        tokens_half = [gather_low(activations), gather_low(far)]
        tokens_all = 2 * tokens_half[0].shape[0]
        scale = 1.0 / tokens_all
        grad_all = lax.all_gather(out_grads, "feat", axis=0, tiled=True)
        out_share = lax.psum_scatter(
            jnp.dot(grad_all, basis_out, preferred_element_type=F32),
            "ex",
            scatter_dimension=0,
            tiled=True,
        )
        rotated_out = lax.all_gather(out_share.astype(BF16), "ex", axis=0, tiled=True)
        out_a, out_b = ordered(rotated_out, y), ordered(rotated_out, side)

        width = 512
        chunks = list(range(0, columns, width))
        lead = 4
        order = [(0, i) for i in range(min(lead, len(chunks)))]
        for i in range(len(chunks)):
            order.append((1, i))
            if i + lead < len(chunks):
                order.append((0, i + lead))
        pieces = {}
        result = None
        for half, i in order:
            first = chunks[i]
            partial = jnp.dot(tokens_half[half], basis_in[:, first : first + width], preferred_element_type=F32)
            if i % 2 == 0:
                pieces[half, i] = tree_a(partial, y, z)
            else:
                pieces[half, i] = tree_b(partial, side, z)
            if half == 1:
                result = square_into(
                    result, out_a if i % 2 == 0 else out_b, pieces[0, i] + pieces[1, i], first, width, columns, scale
                )
        return result

    return per_device


def solution(mesh):
    return jax.shard_map(
        make_per_device(mesh.shape["feat"], mesh.shape["ex"]),
        mesh=mesh,
        in_specs=(P("ex", "feat"), P("feat", "ex"), P("feat", "ex"), P("ex", "feat")),
        out_specs=P("feat", "ex"),
        check_vma=False,
    )
```

```python
import jax
import jax.numpy as jnp
from jax import lax
from jax.experimental import pallas as pl
from jax.experimental.pallas import tpu as pltpu
from jax.sharding import PartitionSpec as P

SEQ_LEN = 256
EXTRA = {0: 1, 1: 1, 2: 1, 3: 1, 4: 1}
PARTS = 4
WIDTH = 256
BF16 = jnp.bfloat16
F32 = jnp.float32


def square_kernel(scale, out_t, p0, p1, p2, p3, *rest):
    result = rest[-1]
    total = None
    for n, piece in enumerate((p0, p1, p2, p3)):
        rows = piece.shape[0]
        for s in range(rows // SEQ_LEN):
            left = out_t[:, n * rows + s * SEQ_LEN : n * rows + (s + 1) * SEQ_LEN]
            right = piece[s * SEQ_LEN : (s + 1) * SEQ_LEN, :]
            product = jnp.dot(left, right, preferred_element_type=F32)
            total = product * product if total is None else total + product * product
    result[...] = total * scale


def square_into(buffer, out_t, pieces, first, width, full, scale):
    tile = 256
    rows = out_t.shape[0]
    depth = pieces[0].shape[0]
    offset = first // tile
    in_specs = [pl.BlockSpec(out_t.shape, lambda j: (0, 0))]
    in_specs += [pl.BlockSpec((depth, tile), lambda j: (0, j)) for _ in pieces]
    operands = [out_t, *pieces]
    aliases = {}
    if buffer is not None:
        in_specs.append(pl.BlockSpec(memory_space=pl.ANY))
        operands.append(buffer)
        aliases = {len(operands) - 1: 0}

    def body(*refs):
        square_kernel(scale, *refs)

    return pl.pallas_call(
        body,
        grid=(width // tile,),
        in_specs=in_specs,
        out_specs=pl.BlockSpec((rows, tile), lambda j: (0, offset + j)),
        out_shape=jax.ShapeDtypeStruct((rows, full), F32),
        input_output_aliases=aliases,
        compiler_params=pltpu.CompilerParams(vmem_limit_bytes=32 * 1024 * 1024),
        cost_estimate=pl.CostEstimate(
            flops=2 * rows * width * out_t.shape[1],
            bytes_accessed=rows * width * 4 + out_t.size * 2 + PARTS * depth * width * 2,
            transcendentals=0,
        ),
    )(*operands)


def call(kernel, flags, operands, in_specs, outputs, out_specs, grid, cost, aliases, vmem):
    return pl.pallas_call(
        kernel,
        grid_spec=pltpu.PrefetchScalarGridSpec(
            num_scalar_prefetch=1, grid=grid, in_specs=in_specs, out_specs=out_specs
        ),
        out_shape=outputs,
        input_output_aliases=aliases or {},
        compiler_params=pltpu.CompilerParams(vmem_limit_bytes=vmem * 1024 * 1024),
        cost_estimate=cost,
    )(flags, *operands)


def unit_list(count):
    lead = 6
    units = [[(0, i)] for i in range(lead)]
    units += [[(1, i), (1, i + 1)] for i in range(0, lead, 2)]
    rest = [(half, i) for i in range(lead, count) for half in (0, 1)]
    while rest:
        size = 2 if len(rest) > 8 else 1
        units.append(rest[:size])
        rest = rest[size:]
    return units


class Chain:
    def __init__(self, flags):
        self.flags = flags
        self.token = jnp.zeros((8, 128), F32)
        self.also = []

    def run(self, body, operands, in_specs, outputs, out_specs, grid, flops, size, aliases=None, vmem=10):
        waits = [self.token, *self.also]
        self.also = []
        count, made = len(operands), len(outputs)
        keep = pl.BlockSpec(memory_space=pl.ANY)

        def kernel(flags, *refs):
            refs[-1][...] = jnp.zeros((8, 128), F32)
            body(flags, refs[:count], refs[count + len(waits) : -1])

        results = call(
            kernel,
            self.flags,
            [*operands, *waits],
            [*in_specs, *[keep] * len(waits)],
            [*outputs, jax.ShapeDtypeStruct((8, 128), F32)],
            [*out_specs, pl.BlockSpec((8, 128), lambda *_: (0, 0))],
            grid,
            pl.CostEstimate(flops=flops, bytes_accessed=size, transcendentals=0),
            aliases,
            vmem,
        )
        self.token = results[made]
        return results[:made]


def multiply(chain, blocks, matrix, first, width, dtype, vmem, tile=256):
    rows = sum(block.shape[0] for block in blocks)
    inner = matrix.shape[0]
    base = first // tile

    def body(flags, ins, outs):
        (result,) = outs
        start = 0
        for block in ins[:-1]:
            here = slice(start, start + block.shape[0])
            start += block.shape[0]
            result[here, :] = jnp.dot(block[...], ins[-1][...], preferred_element_type=F32).astype(dtype)

    return chain.run(
        body,
        [*blocks, matrix],
        [pl.BlockSpec(block.shape, lambda j, flags: (0, 0), pipeline_mode=pl.Buffered(1)) for block in blocks]
        + [pl.BlockSpec((inner, tile), lambda j, flags: (0, base + j))],
        [jax.ShapeDtypeStruct((rows, width), dtype)],
        [pl.BlockSpec((rows, tile), lambda j, flags: (0, j))],
        (width // tile,),
        2 * rows * inner * width,
        2 * inner * (rows + width) + 4 * rows * width,
        vmem=vmem,
    )[0]


def relay(chain, value):
    tile = 128

    def body(flags, ins, outs):
        outs[0][...] = ins[0][...]

    spec = pl.BlockSpec((tile, value.shape[1]), lambda r, flags: (r, 0))
    shape = jax.ShapeDtypeStruct(value.shape, value.dtype)
    return chain.run(body, [value], [spec], [shape], [spec], (value.shape[0] // tile,), 0, 4 * value.size)[0]


def rotate_out(chain, grads, basis):
    inner, width = basis.shape
    tile = 256

    def body(flags, ins, outs):
        for q in range(PARTS):
            rows = pl.ds(pl.multiple_of((flags[3] ^ q) * SEQ_LEN, SEQ_LEN), SEQ_LEN)
            product = jnp.dot(ins[0][rows, :], ins[1][...], preferred_element_type=F32)
            outs[q % 2][q // 2 * SEQ_LEN : (q // 2 + 1) * SEQ_LEN, :] = product

    half = jax.ShapeDtypeStruct((2 * SEQ_LEN, width), F32)
    return chain.run(
        body,
        [grads, basis],
        [
            pl.BlockSpec(grads.shape, lambda j, flags: (0, 0), pipeline_mode=pl.Buffered(1)),
            pl.BlockSpec((inner, tile), lambda j, flags: (0, j)),
        ],
        [half, half],
        [pl.BlockSpec((2 * SEQ_LEN, tile), lambda j, flags: (0, j))] * 2,
        (width // tile,),
        2 * grads.size * width,
        2 * (grads.size + basis.size) + 4 * PARTS * SEQ_LEN * width,
        vmem=14,
    )


def add_rows(chain, mine, other, dtype):
    rows, width = mine.shape
    tile = 256
    count = rows // SEQ_LEN

    def body(flags, ins, outs):
        for n in range(count):
            here = slice(n * SEQ_LEN, (n + 1) * SEQ_LEN)
            outs[n][...] = (ins[0][here, :] + ins[1][here, :]).astype(dtype)

    return chain.run(
        body,
        [mine, other],
        [pl.BlockSpec((rows, tile), lambda j, flags: (0, j))] * 2,
        [jax.ShapeDtypeStruct((SEQ_LEN, width), dtype)] * count,
        [pl.BlockSpec((SEQ_LEN, tile), lambda j, flags: (0, j))] * count,
        (width // tile,),
        0,
        12 * rows * width,
    )


def turn(chain, pieces):
    rows, width = pieces[0].shape
    tile = 256

    def body(flags, ins, outs):
        for q in range(len(pieces)):
            outs[0][q] = ins[q][...].T

    return chain.run(
        body,
        pieces,
        [pl.BlockSpec((rows, tile), lambda j, flags: (0, j))] * len(pieces),
        [jax.ShapeDtypeStruct((len(pieces), width, rows), pieces[0].dtype)],
        [pl.BlockSpec((len(pieces), tile, rows), lambda j, flags: (0, j, 0))],
        (width // tile,),
        0,
        4 * len(pieces) * rows * width,
    )[0]


def layout(parts):
    offsets, total = {}, 0
    for name, rows, present in parts:
        if present:
            offsets[name] = total
            total += rows
    return offsets, total


class Lane:
    def __init__(self, chain, units, permute):
        self.chain, self.units, self.permute = chain, units, permute
        self.sent, self.got, self.state, self.places, self.partials = {}, {}, {}, {}, {}

    def subs(self, u):
        return len(self.units[u]) if 0 <= u < len(self.units) else 0

    def advance(self, k, partials):
        half, n = SEQ_LEN, self.subs
        self.partials[k] = partials
        places, sizes = {}, {}
        for link, parts in (
            ("y", (("a1", half, n(k)), ("a5", half, n(k - 4)), ("b3", half, n(k - 2)))),
            ("z", (("za", half, max(n(k - 1), n(k - 3))), ("zb", 2 * half, max(n(k), n(k - 4))))),
            ("m", (("a3", half, n(k - 2)), ("b2", half, n(k - 1)), ("b4", half, n(k - 3)))),
        ):
            places[link], sizes[link] = layout([(name, rows * count, count) for name, rows, count in parts])
        before = self.places
        operands, in_specs, names, outputs, out_specs, out_names = [], [], [], [], [], []
        size = 0

        def read(name, array, rows=None, block=0, first=0):
            nonlocal size
            rows = rows or array.shape[0]
            base = first // 128
            operands.append(array)
            in_specs.append(pl.BlockSpec((rows, 128), lambda j, flags: (block, base + j)))
            names.append(name)
            size += rows * WIDTH * array.dtype.itemsize

        def write(name, rows, dtype):
            nonlocal size
            outputs.append(jax.ShapeDtypeStruct((rows, WIDTH), dtype))
            out_specs.append(pl.BlockSpec((rows, 128), lambda j, flags: (0, j)))
            out_names.append(name)
            size += rows * WIDTH * jnp.dtype(dtype).itemsize

        for link, array in self.got.items():
            read("got_" + link, array)
        for link, array in self.sent.items():
            if (link == "z" and (n(k - 4) or n(k - 5))) or (link == "m" and n(k - 4)):
                read("sent_" + link, array)
        for age in (0, 1):
            for s in range(n(k - age)):
                array, block, first = self.partials[k - age][s]
                read(f"p{age}a{s}", array, 2 * half, block, first)
                read(f"p{age}b{s}", array, 2 * half, block, first + WIDTH)
        for name, u in (("a1", k - 2), ("b1", k - 2), ("a2", k - 3), ("b2", k - 3)):
            if n(u):
                read("old_" + name, self.state[name])
        for link, rows in sizes.items():
            if rows:
                write("out_" + link, rows, BF16)
        for name, u in (("a1", k - 1), ("b1", k - 1), ("a2", k - 2), ("b2", k - 2)):
            if n(u):
                write("new_" + name, half * n(u), F32)
        if n(k - 5):
            write("final", 2 * half * n(k - 5), BF16)

        def body(flags, ins, outs):
            refs = dict(zip(names + out_names, (*ins, *outs)))
            y, side, outer = flags[0], flags[1], flags[2] == 1

            def rows(start, count=half):
                return pl.ds(pl.multiple_of(start, 16), count)

            def put(link, part, value, extra=0):
                start = places[link][part] + extra
                refs["out_" + link][start : start + value.shape[0], :] = value.astype(BF16)

            def take(kind, link, part, extra=0, count=half):
                return refs[kind + "_" + link][rows(before[link][part] + extra, count), :]

            for s in range(n(k)):
                put("y", "a1", refs[f"p0a{s}"][rows((1 - y) * half), :], s * half)
            for s in range(n(k - 1)):
                total = refs[f"p1a{s}"][rows(y * half), :].astype(F32) + take("got", "y", "a1", s * half).astype(F32)
                refs["new_a1"][s * half : (s + 1) * half, :] = total

            @pl.when(outer)
            def _():
                for s in range(n(k)):
                    put("z", "zb", refs[f"p0b{s}"][...], s * 2 * half)
                if n(k - 1):
                    put("z", "za", refs["new_a1"][...])
                if n(k - 4):
                    put("y", "a5", take("got", "z", "za", 0, half * n(k - 4)))
                if n(k - 5):
                    refs["final"][...] = take("got", "z", "zb", 0, 2 * half * n(k - 5))

            @pl.when(jnp.logical_not(outer))
            def _():
                for s in range(n(k - 1)):
                    for keep, start in ((False, (1 - side) * half), (True, side * half)):
                        value = refs[f"p1b{s}"][rows(start), :].astype(F32)
                        value += take("got", "z", "zb", start + s * 2 * half).astype(F32)
                        if keep:
                            refs["new_b1"][s * half : (s + 1) * half, :] = value
                        else:
                            put("m", "b2", value, s * half)
                if n(k - 2):
                    whole = half * n(k - 2)
                    total = refs["old_a1"][...] + take("got", "z", "za", 0, whole).astype(F32)
                    put("m", "a3", total)
                    refs["new_a2"][...] = total
                    total = refs["old_b1"][...] + take("got", "m", "b2", 0, whole).astype(F32)
                    put("y", "b3", total)
                    refs["new_b2"][...] = total
                if n(k - 3):
                    whole = half * n(k - 3)
                    put("z", "za", refs["old_a2"][...] + take("got", "m", "a3", 0, whole).astype(F32))
                    put("m", "b4", refs["old_b2"][...] + take("got", "y", "b3", 0, whole).astype(F32))
                if n(k - 4):
                    put("y", "a5", take("sent", "z", "za", 0, half * n(k - 4)))
                for s in range(n(k - 4)):
                    put("z", "zb", take("sent", "m", "b4", s * half), s * 2 * half)
                    put("z", "zb", take("got", "m", "b4", s * half), s * 2 * half + half)
                if n(k - 5):
                    refs["final"][...] = take("sent", "z", "zb", 0, 2 * half * n(k - 5))

        made = self.chain.run(body, operands, in_specs, outputs, out_specs, (WIDTH // 128,), 0, size, vmem=4 + size // 2**20)
        made = dict(zip(out_names, made))
        ready = []
        for s in range(n(k - 5)):
            place = before["y"]["a5"] // half + s
            ready.append((self.units[k - 5][s], (self.sent["y"], self.got["y"], place, made["final"], s)))
        self.places = places
        self.sent = {link: made["out_" + link] for link in sizes if sizes[link]}
        self.got = {link: self.permute[link](value) for link, value in self.sent.items()}
        self.state = {name[4:]: value for name, value in made.items() if name.startswith("new_")}
        return ready


def square_chunk(chain, buffer, out_t, pair, index, full, scale):
    rows = out_t.shape[1]
    tile = 512
    operands, in_specs = [out_t], [pl.BlockSpec((PARTS, tile, SEQ_LEN), lambda r, flags: (0, r, 0))]
    for own, other, place, _, _ in pair:
        for array in (own, other):
            operands.append(array)
            in_specs.append(pl.BlockSpec((SEQ_LEN, WIDTH), lambda r, flags, place=place: (place, 0)))
    for *_, final, s in pair:
        operands.append(final)
        in_specs.append(pl.BlockSpec((2 * SEQ_LEN, WIDTH), lambda r, flags, s=s: (s, 0)))
    aliases = {}
    if buffer is not None:
        in_specs.append(pl.BlockSpec(memory_space=pl.ANY))
        operands.append(buffer)
        aliases = {len(operands): 0}

    def body(flags, ins, outs):
        y, side = flags[0], flags[1]
        left, a, b = ins[0], ins[1:5], ins[5:7]
        (result,) = outs

        def square(seq, right):
            product = jnp.dot(left[seq], right, preferred_element_type=F32)
            return product * product

        total = square(y, a[0][...]) + square(1 - y, a[1][...])
        total += square(2 + y, a[2][...]) + square(3 - y, a[3][...])
        result[:, :WIDTH] = total * scale
        total = square(side, b[0][:SEQ_LEN, :]) + square(1 - side, b[0][SEQ_LEN:, :])
        total += square(2 + side, b[1][:SEQ_LEN, :]) + square(3 - side, b[1][SEQ_LEN:, :])
        result[:, WIDTH:] = total * scale

    return chain.run(
        body,
        operands,
        in_specs,
        [jax.ShapeDtypeStruct((rows, full), F32)],
        [pl.BlockSpec((tile, 2 * WIDTH), lambda r, flags: (r, index))],
        (rows // tile,),
        4 * rows * WIDTH * PARTS * SEQ_LEN,
        rows * WIDTH * 8 + out_t.size * 2 + PARTS * SEQ_LEN * WIDTH * 4,
        aliases,
    )[0]


def make_per_device(feat, ex):
    depth = feat // 2
    mid = depth // 2

    def along_z(pairs):
        return [(a * 2 + y, b * 2 + y) for a, b in pairs for y in (0, 1)]

    inward = [along_z([(k, k + 1), (depth - 1 - k, depth - 2 - k)]) for k in range(mid - 1)]
    outward = [along_z([(k + 1, k), (depth - 2 - k, depth - 1 - k)]) for k in reversed(range(mid - 1))]
    middle = along_z([(mid - 1, mid), (mid, mid - 1)])
    y_swap = [(i, i ^ 1) for i in range(feat)]
    y_middle = [(i, i ^ 1) for i in range(feat) if i // 2 in (mid - 1, mid)]

    def swap_ex(value, bit):
        return lax.ppermute(value, "ex", [(i, i ^ bit) for i in range(ex)])

    def send(value, pairs):
        return lax.ppermute(value.astype(BF16), "feat", pairs)

    def gather_low(block):
        bit = 1
        while bit < ex // 2:
            block = jnp.concatenate([block, swap_ex(block, bit)], axis=0)
            bit *= 2
        return block

    def spread(value, z):
        for step, pairs in enumerate(outward):
            level = mid - 2 - step
            here = (z == level) | (z == depth - 1 - level)
            value = jnp.where(here, lax.ppermute(value, "feat", pairs), value)
        return value

    def tree_a(partial, y, z):
        half = partial.shape[0] // 2
        away = lax.dynamic_slice_in_dim(partial, (1 - y) * half, half, 0)
        total = lax.dynamic_slice_in_dim(partial, y * half, half, 0)
        total = total + send(away, y_swap).astype(F32)
        for pairs in inward:
            total = total + send(total, pairs).astype(F32)
        total = (total + send(total, middle).astype(F32)).astype(BF16)
        total = spread(total, z)
        return [total, lax.ppermute(total, "feat", y_swap)]

    def tree_b(partial, side, z):
        half = partial.shape[0] // 2
        for pairs in inward:
            partial = partial + send(partial, pairs).astype(F32)
        away = lax.dynamic_slice_in_dim(partial, (1 - side) * half, half, 0)
        total = lax.dynamic_slice_in_dim(partial, side * half, half, 0)
        total = total + send(away, middle).astype(F32)
        total = (total + send(total, y_middle).astype(F32)).astype(BF16)
        other = lax.ppermute(total, "feat", middle)
        return [spread(total, z), spread(other, z)]

    def pipelined(activations, out_grads, basis_in, basis_out, flags):
        columns = basis_in.shape[1]
        chain = Chain(flags)
        stay = [(k, k) for k in range(feat) if k // 2 in (0, depth - 1)]
        permute = {
            "y": lambda v: lax.ppermute(v, "feat", y_swap),
            "z": lambda v: lax.ppermute(v, "feat", inward[0] + outward[0]),
            "m": lambda v: lax.ppermute(v, "feat", middle + stay),
        }
        near = [activations, swap_ex(activations, 1)]
        far = swap_ex(activations, 2)
        grad_all = lax.all_gather(out_grads, "feat", axis=0, tiled=True)
        tokens_all = PARTS * activations.shape[0]
        tokens = [near, None]

        count = columns // (2 * WIDTH)
        units = unit_list(count)
        lanes = [Lane(chain, units[p::2], permute) for p in (0, 1)]
        finished, made, waiting = {}, {}, []

        def square(result, i):
            pair = (finished[0, i], finished[1, i])
            return square_chunk(chain, result, out_t, pair, i, columns, 1.0 / tokens_all)

        result = out_t = None
        for j in range(len(units) + 12):
            lane, k = lanes[j % 2], j // 2
            if k >= len(lane.units) + 6:
                continue
            partials = None
            if lane.subs(k):
                unit = lane.units[k]
                if tokens[1] is None and j == 4:
                    far = relay(chain, far)
                    tokens[1] = [far, swap_ex(far, 1)]
                if unit[0] not in made:
                    group = list(unit)
                    if j + 1 < len(units) and len({half for half, _ in unit + units[j + 1]}) == len(unit) == 2:
                        if len({i for _, i in unit}) == 1:
                            group += units[j + 1]
                    halves = sorted({half for half, _ in group})
                    chunks = sorted({i for _, i in group})
                    blocks = [block for half in halves for block in tokens[half]]
                    wide = 2 * WIDTH * len(chunks)
                    array = multiply(chain, blocks, basis_in, chunks[0] * 2 * WIDTH, wide, BF16, 8 if len(blocks) == 2 else 14)
                    for half, i in group:
                        made[half, i] = (array, halves.index(half), chunks.index(i) * 2 * WIDTH)
                partials = [made[sub] for sub in unit]
            ready = lane.advance(k, partials)
            other = lanes[1 - j % 2].got
            spare = len(lane.got) + len(other) + EXTRA.get(j, 0) - 5
            chain.also += [other[link] for link in "myz" if link in other][: max(spare, 0)]
            if j == 9:
                keep, away = rotate_out(chain, grad_all, basis_out)
                away = swap_ex(away, 1)
            if j == 10:
                keep, away = add_rows(chain, keep, away, F32)
                away = swap_ex(away, 2)
            if j == 13:
                (own,) = add_rows(chain, keep, away, BF16)
                across = swap_ex(own, 2)
                beside = [swap_ex(own, 1), swap_ex(across, 1)]
            if j == 15:
                out_t = turn(chain, [own, beside[0], across, beside[1]])
            for (half, i), value in ready:
                finished[half, i] = value
                if (1 - half, i) in finished:
                    waiting.append(i)
            if waiting and out_t is not None:
                result = square(result, waiting.pop(0))
        for i in waiting:
            result = square(result, i)
        return result

    def per_device(activations, out_grads, basis_in, basis_out):
        place = lax.axis_index("feat")
        e = lax.axis_index("ex")
        y, z = place % 2, place // 2
        side = (z >= mid).astype(jnp.int32)
        columns = basis_in.shape[1]

        block = activations.shape[0]

        def ordered(rotated_out, flip):
            turned = []
            for q in range(PARTS):
                for r in range(ex // PARTS):
                    source = e ^ ((q ^ flip) * (ex // PARTS) + r)
                    turned.append(lax.dynamic_slice_in_dim(rotated_out, source * block, block, 0))
            return jnp.concatenate(turned, axis=0).T

        if depth == 4 and ex == PARTS and block == SEQ_LEN and columns % (2 * WIDTH) == 0:
            outer = ((z == 0) | (z == depth - 1)).astype(jnp.int32)
            flags = jnp.stack([y.astype(jnp.int32), side, outer, e.astype(jnp.int32)])
            return pipelined(activations, out_grads, basis_in, basis_out, flags)

        far = swap_ex(activations, ex // 2)
        tokens_half = [gather_low(activations), gather_low(far)]
        tokens_all = 2 * tokens_half[0].shape[0]
        scale = 1.0 / tokens_all
        grad_all = lax.all_gather(out_grads, "feat", axis=0, tiled=True)
        out_share = lax.psum_scatter(
            jnp.dot(grad_all, basis_out, preferred_element_type=F32),
            "ex",
            scatter_dimension=0,
            tiled=True,
        )
        rotated_out = lax.all_gather(out_share.astype(BF16), "ex", axis=0, tiled=True)
        out_a, out_b = ordered(rotated_out, y), ordered(rotated_out, side)

        width = 512
        chunks = list(range(0, columns, width))
        lead = 4
        order = [(0, i) for i in range(min(lead, len(chunks)))]
        for i in range(len(chunks)):
            order.append((1, i))
            if i + lead < len(chunks):
                order.append((0, i + lead))
        pieces = {}
        result = None
        for half, i in order:
            first = chunks[i]
            partial = jnp.dot(tokens_half[half], basis_in[:, first : first + width], preferred_element_type=F32)
            if i % 2 == 0:
                pieces[half, i] = tree_a(partial, y, z)
            else:
                pieces[half, i] = tree_b(partial, side, z)
            if half == 1:
                result = square_into(
                    result, out_a if i % 2 == 0 else out_b, pieces[0, i] + pieces[1, i], first, width, columns, scale
                )
        return result

    return per_device


def solution(mesh):
    return jax.shard_map(
        make_per_device(mesh.shape["feat"], mesh.shape["ex"]),
        mesh=mesh,
        in_specs=(P("ex", "feat"), P("feat", "ex"), P("feat", "ex"), P("ex", "feat")),
        out_specs=P("feat", "ex"),
        check_vma=False,
    )
```
